32 devices in a mesh: pair: 4 (over x, core), ints: 8 (over z, y).
Axes of the slice: x: 2, y: 2, z: 4, core: 2. Of those that a mesh axis runs over, the one named last changes fastest.
Arguments:
- t2: bfloat16 [2048, 4096], P('pair', 'ints'), may hold values from -6 to 6
- t2_live: int32 [4, 32], P('pair', 'ints'), may hold values 0 or 1
- int_tiles: int32 [2560, 2], P('ints'), may hold values from 0 to 31
- integrals: bfloat16 [2560, 128, 128], P('ints'), may hold values from -0.0625 to 0.0625
- cycle_w: bfloat16 [2048, 2048], P('pair'), may hold values from -0.125 to 0.125
- res_live: int32 [4, 32], P('pair', 'ints'), may hold values 0 or 1
Outputs:
- residual: float32 [2048, 4096], P('pair', 'ints')
The draws below stay inside these ranges and needn't reach their ends.
All inputs are finite; a program needn't handle non-finite values. No bound on the sum of `t2_live` or of `res_live` on one device may be relied on, other than what follows from the above.
Results may differ from the reference program's by a relative error of at most 0.0003.
Values may be sent and summed in bfloat16 or wider, within the bound.
A program may use at most 192 MiB of HBM per device.

```python
import jax
import jax.numpy as jnp
from jax import lax

TILE = 128
NT_DEV = 4
VI_DEV = 320
NBLK = 4
PAIRS = 2048
NT = 32
NV = 2560


def touch_ends(values, own_key, least, high):
    place = [jax.random.randint(jax.random.fold_in(own_key, axis), (), 0, length) for axis, length in enumerate(values.shape)]
    main_axis = values.shape.index(max(values.shape))
    neighbour = place[:main_axis] + [(place[main_axis] + 1) % values.shape[main_axis]] + place[main_axis + 1:]
    return values.at[tuple(place)].set(least).at[tuple(neighbour)].set(high)


def levels(own_key, extent, pieces, smallest, top_value):
    factor_of = 1.0
    for axis_at, blocks in pieces:
        draws = jax.random.uniform(jax.random.fold_in(jax.random.fold_in(own_key, 6), axis_at), (blocks,), jnp.float32, smallest / len(pieces), top_value / len(pieces))
        factor_of = factor_of * jnp.repeat(jnp.exp(draws), extent[axis_at] // blocks).reshape((-1,) + (1,) * (len(extent) - 1 - axis_at))
    return factor_of


def noise(stream_key, extent, scale, bound, cuts=(), kind=jnp.bfloat16):
    array = jax.random.normal(stream_key, extent, jnp.float32) * scale
    if len(cuts) > 0:
        array = levels(stream_key, extent, cuts, -0.22, 0.18) * array
    return jnp.clip(array, min=-bound, max=bound).astype(kind)


def setup_inputs(seed: int = 0) -> dict:
    key_list = jax.random.split(jax.random.key(seed), 7)
    t2 = noise(key_list[0], (PAIRS, NT * TILE), 1.0, 6.0, ((0, 4), (1, 8)))
    t2_live = touch_ends((jax.random.randint(key_list[1], (NBLK, NT), 0, 4) < 3).astype(jnp.int32), jax.random.fold_in(key_list[1], 1), 0, 1)
    int_tiles = touch_ends(jax.random.randint(key_list[2], (NV, 2), 0, NT), jax.random.fold_in(key_list[2], 1), 0, NT - 1).astype(jnp.int32)
    integrals = noise(key_list[3], (NV, TILE, TILE), (TILE * VI_DEV // NT_DEV) ** -0.5, 0.0625, ((0, 8),))
    cycle_w = noise(key_list[4], (PAIRS, PAIRS), PAIRS ** -0.5, 0.125, ((0, 4),))
    res_live = touch_ends((jax.random.randint(key_list[5], (NBLK, NT), 0, 4) < 3).astype(jnp.int32), jax.random.fold_in(key_list[5], 1), 0, 1)
    return {"t2": t2, "t2_live": t2_live, "int_tiles": int_tiles, "integrals": integrals, "cycle_w": cycle_w, "res_live": res_live}


def reference(t2, t2_live, int_tiles, integrals, cycle_w, res_live):
    pair_count = t2.shape[0]
    block_rows = pair_count // t2_live.shape[0]
    live_rows = jnp.repeat(t2_live, block_rows, axis=0).astype(t2.dtype)
    amps_tiled = t2.reshape(pair_count, NT, TILE) * live_rows[:, :, None]
    group_size = 64 if VI_DEV % 64 == 0 else VI_DEV
    all_tiles = int_tiles.reshape(NV // group_size, group_size, 2)
    all_ints = integrals.reshape(NV // group_size, group_size, TILE, TILE)

    def ladder_step(partial_value, entry):
        pairs_uv, blocks = entry
        picked = jnp.take(amps_tiled, pairs_uv[:, 0].astype(jnp.int32), axis=1)
        product = jnp.einsum("pjc,jcd->jpd", picked.astype(jnp.float32), blocks.astype(jnp.float32))
        partial_value = partial_value.at[pairs_uv[:, 1].astype(jnp.int32)].add(product)
        return partial_value, None

    total_start = jnp.zeros((NT, pair_count, TILE), jnp.float32)
    total, _ = lax.scan(ladder_step, total_start, (all_tiles, all_ints))
    ladder = total.transpose(1, 0, 2).reshape(pair_count, NT * TILE)
    cycle_term = jnp.dot(cycle_w, amps_tiled.reshape(pair_count, NT * TILE), preferred_element_type=jnp.float32)
    keep_rows = jnp.repeat(res_live, block_rows, axis=0)
    keep_mask = jnp.repeat(keep_rows, TILE, axis=1).astype(jnp.float32)
    return keep_mask * (ladder + cycle_term)
```

```python
import functools

import jax
import jax.numpy as jnp
from jax import lax
from jax.experimental import pallas as pl
from jax.experimental.pallas import tpu as pltpu
from jax.sharding import PartitionSpec as P

MESH = pl.DeviceIdType.MESH
QROWS = 64
QMAX = 32766.0
GROUP = 4
F32 = jnp.float32


def ring_place(index, n):
    inner = index % 2
    outer = index // 2
    return (1 - inner) * outer + inner * (n - 1 - outer)


def ring_index(place, n):
    place = (place + 2 * n) % n
    half = place // (n // 2)
    return (1 - half) * (2 * place) + half * (2 * (n - 1 - place) + 1)


def enter(n, pairs):
    me = lax.axis_index("ints")
    own_pair = lax.axis_index("pair")
    place = ring_place(me, n)
    nexts = (ring_index(place + 1, n), ring_index(place + n - 1, n))
    barrier = pltpu.get_barrier_semaphore()
    for other in nexts:
        pl.semaphore_signal(barrier, inc=1, device_id=(own_pair, other), device_id_type=MESH)
    for step in range(1, pairs):
        peer = (own_pair + step) % pairs
        pl.semaphore_signal(barrier, inc=1, device_id=(peer, me), device_id_type=MESH)
    pl.semaphore_wait(barrier, 2 + max(pairs - 1, 0))
    return me, own_pair, place, nexts


def gather_kernel(n, pairs, tiles, live_ref, t2_ref, w_ref, all_ref, cycle_ref, own, blocks,
                  send_sem, recv_sem, psend_sem, precv_sem, local_sem):
    rows = t2_ref.shape[0]
    width = t2_ref.shape[1] // tiles
    me, own_pair, place, nexts = enter(n, pairs)
    for t in range(tiles):
        keep = live_ref[0, t].astype(F32)
        own[t] = (t2_ref[:, t * width:(t + 1) * width].astype(F32) * keep).astype(own.dtype)

    def copy_of(step, t):
        way = t * 2 // tiles
        sign = 1 - 2 * way
        slot = ring_index(place + n - sign * step, n) * tiles + t
        return pltpu.make_async_remote_copy(
            src_ref=own.at[t] if step == 0 else all_ref.at[slot],
            dst_ref=all_ref.at[slot],
            send_sem=send_sem.at[t, step],
            recv_sem=recv_sem.at[t, step],
            device_id=(own_pair, nexts[way]),
            device_id_type=MESH,
        )

    half = tiles // 2
    order = [t for c in range(half) for t in (c, half + c)]
    flying = {}
    for t in order:
        flying[t, 0] = copy_of(0, t)
        flying[t, 0].start()
    others = []
    for step in range(1, pairs):
        peer = (own_pair + step) % pairs
        c = pltpu.make_async_remote_copy(
            src_ref=own,
            dst_ref=blocks.at[step],
            send_sem=psend_sem.at[step],
            recv_sem=precv_sem.at[step],
            device_id=(peer, me),
            device_id_type=MESH,
        )
        c.start()
        others.append(c)
    mine = pltpu.make_async_copy(own, all_ref.at[pl.ds(me * tiles, tiles)], local_sem)
    mine.start()

    def add_block(step):
        source = (own_pair + pairs - step) % pairs
        left = w_ref[:, pl.ds(pl.multiple_of(source * rows, 128), rows)]
        for t in range(tiles):
            right = own[t] if step == 0 else blocks[step, t]
            part = jnp.dot(left, right, preferred_element_type=F32)
            if step == 0:
                cycle_ref[t] = part
            else:
                cycle_ref[t] += part

    add_block(0)
    for step in range(1, n - 1):
        for t in order:
            flying[t, step - 1].wait_recv()
            flying[t, step] = copy_of(step, t)
            flying[t, step].start()
        if step == n - 2:
            for k in range(1, pairs):
                others[k - 1].wait_recv()
                add_block(k)
    for t in order:
        flying[t, n - 2].wait_recv()
    for c in flying.values():
        c.wait_send()
    for c in others:
        c.wait_send()
    mine.wait()


def ladder_kernel(table_ref, target_ref, count_ref, amps_ref, ints_ref, out_ref, held, sem):
    count = ints_ref.shape[0]
    load = pltpu.make_async_copy(ints_ref, held.at[pl.ds(0, count)], sem)
    load.start()
    held[count] = jnp.zeros(held.shape[1:], held.dtype)
    load.wait()

    def step(s, last):
        target = target_ref[s]
        first = target != last
        picks = [table_ref[0, s * GROUP + g] for g in range(GROUP)]
        sources = [table_ref[1, s * GROUP + g] for g in range(GROUP)]
        left = jnp.concatenate([amps_ref[u] for u in sources], axis=1)
        right = jnp.concatenate([held[j] for j in picks], axis=0)
        part = jnp.dot(left, right, preferred_element_type=F32)

        @pl.when(first)
        def _():
            out_ref[target] = part

        @pl.when(jnp.logical_not(first))
        def _():
            out_ref[target] += part

        return target

    lax.fori_loop(0, count_ref[0], step, jnp.int32(-1))


def reduce_kernel(n, pairs, tiles, keep_ref, cycle_ref, part_ref, out_ref, held, sent, sent_scale,
                  got, got_scale, load_sem, send_sem, recv_sem, ssend_sem, srecv_sem):
    rows = cycle_ref.shape[1]
    width = cycle_ref.shape[2]
    chunks = rows // QROWS
    half = tiles // 2
    order = [t for c in range(half) for t in (c, half + c)]
    own_pair = lax.axis_index("pair")
    place = ring_place(lax.axis_index("ints"), n)

    def slot_of(step, t):
        sign = 1 - 2 * (t * 2 // tiles)
        return ring_index(place + 2 * n - sign * (step + 1), n) * tiles + t

    loads = {}
    for step in range(n):
        for t in order:
            loads[t, step] = pltpu.make_async_copy(
                part_ref.at[slot_of(step, t)], held.at[t, step], load_sem.at[t, step]
            )
            loads[t, step].start()
    me, own_pair, place, nexts = enter(n, 1)

    def total(step, t, k):
        at = pl.ds(pl.multiple_of(k * QROWS, QROWS), QROWS)
        value = held[t, step, at, :]
        if step > 0:
            scale = got_scale[t, step - 1, pl.ds(k, 1), :]
            value = value + got[t, step - 1, at, :].astype(jnp.int32).astype(F32) * scale
        return at, value

    def pack(step, t):
        def body(k, carry):
            at, value = total(step, t, k)
            top = jnp.maximum(jnp.max(jnp.abs(value), axis=0, keepdims=True), 1e-30)
            sent_scale[t, step, pl.ds(k, 1), :] = top * (1.0 / QMAX)
            scaled = jnp.round(value * (QMAX / top))
            sent[t, step, at, :] = scaled.astype(jnp.int32).astype(jnp.int16)
            return carry

        lax.fori_loop(0, chunks, body, 0)

    def copies(step, t):
        way = t * 2 // tiles
        where = (own_pair, nexts[way])
        return [
            pltpu.make_async_remote_copy(
                src_ref=a.at[t, step], dst_ref=b.at[t, step], send_sem=c.at[t, step],
                recv_sem=d.at[t, step], device_id=where, device_id_type=MESH,
            )
            for a, b, c, d in (
                (sent, got, send_sem, recv_sem),
                (sent_scale, got_scale, ssend_sem, srecv_sem),
            )
        ]

    flying = {}
    for step in range(n - 1):
        for t in order:
            loads[t, step].wait()
            if step > 0:
                for c in flying[t, step - 1]:
                    c.wait_recv()
            pack(step, t)
            flying[t, step] = copies(step, t)
            for c in flying[t, step]:
                c.start()
    for t in order:
        loads[t, n - 1].wait()
        for c in flying[t, n - 2]:
            c.wait_recv()
        keep = keep_ref[0, t].astype(F32)

        def body(k, carry):
            at, value = total(n - 1, t, k)
            out_ref[at, t * width:(t + 1) * width] = (value + cycle_ref[t, at, :]) * keep
            return carry

        lax.fori_loop(0, chunks, body, 0)
    for pair_of in flying.values():
        for c in pair_of:
            c.wait_send()


def tables(int_tiles, tiles_all):
    count = int_tiles.shape[0]
    slots = (count + GROUP * tiles_all) // GROUP
    u, v = int_tiles[:, 0], int_tiles[:, 1]
    ids = jnp.arange(count, dtype=jnp.int32)
    tile_ids = jnp.arange(tiles_all, dtype=jnp.int32)
    rank = jnp.sum((v[:, None] == v[None, :]) & (ids[None, :] < ids[:, None]), axis=1, dtype=jnp.int32)
    counts = jnp.sum(v[:, None] == tile_ids[None, :], axis=0, dtype=jnp.int32)
    groups = jnp.maximum((counts + GROUP - 1) // GROUP, 1)
    ends = jnp.sum(jnp.where(tile_ids[:, None] >= tile_ids[None, :], groups[None, :], 0), axis=1)
    base = jnp.sum(jnp.where(tile_ids[None, :] < v[:, None], groups[None, :], 0), axis=1)
    spot = base * GROUP + rank
    hit = spot[None, :] == jnp.arange(slots * GROUP, dtype=jnp.int32)[:, None]
    picks = count + jnp.sum(jnp.where(hit, ids[None, :] - count, 0), axis=1)
    sources = jnp.sum(jnp.where(hit, u[None, :], 0), axis=1)
    target = jnp.sum(ends[None, :] <= jnp.arange(slots, dtype=jnp.int32)[:, None], axis=1, dtype=jnp.int32)
    return jnp.stack([picks, sources]), target, ends[-1:]


def vmem():
    return pl.BlockSpec(memory_space=pltpu.VMEM)


def smem():
    return pl.BlockSpec(memory_space=pltpu.SMEM)


def anywhere():
    return pl.BlockSpec(memory_space=pl.ANY)


def local(n, pairs, t2, t2_live, int_tiles, integrals, cycle_w, res_live):
    rows = t2.shape[0]
    width = integrals.shape[1]
    tiles = t2.shape[1] // width
    tiles_all = tiles * n
    count = integrals.shape[0]
    dma = pltpu.SemaphoreType.DMA
    amps, cycle = pl.pallas_call(
        functools.partial(gather_kernel, n, pairs, tiles),
        out_shape=(
            jax.ShapeDtypeStruct((tiles_all, rows, width), t2.dtype),
            jax.ShapeDtypeStruct((tiles, rows, width), F32),
        ),
        in_specs=[smem(), vmem(), vmem()],
        out_specs=(anywhere(), vmem()),
        scratch_shapes=[
            pltpu.VMEM((tiles, rows, width), t2.dtype),
            pltpu.VMEM((pairs, tiles, rows, width), t2.dtype),
            dma((tiles, n)), dma((tiles, n)), dma((pairs,)), dma((pairs,)), dma,
        ],
        compiler_params=pltpu.CompilerParams(
            collective_id=0, has_side_effects=True, vmem_limit_bytes=48 << 20
        ),
        name="gather_amps",
    )(t2_live, t2, cycle_w)

    table, target, steps = tables(int_tiles, tiles_all)
    partial = pl.pallas_call(
        ladder_kernel,
        out_shape=jax.ShapeDtypeStruct((tiles_all, rows, width), F32),
        in_specs=[smem(), smem(), smem(), vmem(), anywhere()],
        out_specs=vmem(),
        scratch_shapes=[pltpu.VMEM((count + 1, width, width), integrals.dtype), dma],
        compiler_params=pltpu.CompilerParams(vmem_limit_bytes=56 << 20),
        name="ladder_partial",
    )(table, target, steps, amps, integrals)

    chunks = rows // QROWS
    return pl.pallas_call(
        functools.partial(reduce_kernel, n, pairs, tiles),
        out_shape=jax.ShapeDtypeStruct((rows, tiles * width), F32),
        in_specs=[smem(), vmem(), anywhere()],
        out_specs=vmem(),
        scratch_shapes=[
            pltpu.VMEM((tiles, n, rows, width), F32),
            pltpu.VMEM((tiles, n - 1, rows, width), jnp.int16),
            pltpu.VMEM((tiles, n - 1, chunks, width), F32),
            pltpu.VMEM((tiles, n - 1, rows, width), jnp.int16),
            pltpu.VMEM((tiles, n - 1, chunks, width), F32),
            dma((tiles, n)), dma((tiles, n)), dma((tiles, n)), dma((tiles, n)), dma((tiles, n)),
        ],
        compiler_params=pltpu.CompilerParams(
            collective_id=1, has_side_effects=True, vmem_limit_bytes=56 << 20
        ),
        name="reduce_partial",
    )(res_live, cycle, partial)


def solution(mesh):
    n = mesh.shape["ints"]
    pairs = mesh.shape["pair"]
    placed = (
        P("pair", "ints"),
        P("pair", "ints"),
        P("ints", None),
        P("ints", None, None),
        P("pair", None),
        P("pair", "ints"),
    )
    return jax.shard_map(
        functools.partial(local, n, pairs), mesh=mesh, in_specs=placed,
        out_specs=P("pair", "ints"), check_vma=False
    )
```

```python
import functools

import jax
import jax.numpy as jnp
from jax import lax
from jax.experimental import pallas as pl
from jax.experimental.pallas import tpu as pltpu
from jax.sharding import PartitionSpec as P

MESH = pl.DeviceIdType.MESH
QROWS = 64
QMAX = 32766.0
GROUP = 4
UNROLL = 4
PHASE = 4
F32 = jnp.float32


def ring_place(index, n):
    inner = index % 2
    outer = index // 2
    return (1 - inner) * outer + inner * (n - 1 - outer)


def ring_index(place, n):
    place = (place + 2 * n) % n
    half = place // (n // 2)
    return (1 - half) * (2 * place) + half * (2 * (n - 1 - place) + 1)


def enter(n, pairs):
    me = lax.axis_index("ints")
    own_pair = lax.axis_index("pair")
    place = ring_place(me, n)
    nexts = (ring_index(place + 1, n), ring_index(place + n - 1, n))
    barrier = pltpu.get_barrier_semaphore()
    for other in nexts:
        pl.semaphore_signal(barrier, inc=1, device_id=(own_pair, other), device_id_type=MESH)
    for step in range(1, pairs):
        peer = (own_pair + step) % pairs
        pl.semaphore_signal(barrier, inc=1, device_id=(peer, me), device_id_type=MESH)
    pl.semaphore_wait(barrier, 2 + max(pairs - 1, 0))
    return me, own_pair, place, nexts


def gather_kernel(n, pairs, tiles, live_ref, t2_hbm, w_hbm, all_ref, cycle_hbm, own, blocks, t2_ref,
                  w_ref, cycle_ref, send_sem, recv_sem, psend_sem, precv_sem, local_sem):
    rows = t2_ref.shape[0]
    width = t2_ref.shape[1] // tiles
    t2_load = pltpu.make_async_copy(t2_hbm, t2_ref, local_sem.at[1])
    t2_load.start()
    w_load = pltpu.make_async_copy(w_hbm, w_ref, local_sem.at[2])
    w_load.start()
    me, own_pair, place, nexts = enter(n, pairs)
    t2_load.wait()
    for t in range(tiles):
        keep = live_ref[0, t].astype(F32)
        own[t] = (t2_ref[:, t * width:(t + 1) * width].astype(F32) * keep).astype(own.dtype)

    def copy_of(step, t):
        way = t * 2 // tiles
        sign = 1 - 2 * way
        slot = ring_index(place + n - sign * step, n) * tiles + t
        return pltpu.make_async_remote_copy(
            src_ref=own.at[t] if step == 0 else all_ref.at[slot],
            dst_ref=all_ref.at[slot],
            send_sem=send_sem.at[t, step],
            recv_sem=recv_sem.at[t, step],
            device_id=(own_pair, nexts[way]),
            device_id_type=MESH,
        )

    half = tiles // 2
    order = [t for c in range(half) for t in (c, half + c)]
    flying = {}
    for t in order:
        flying[t, 0] = copy_of(0, t)
        flying[t, 0].start()
    others = []
    for step in range(1, pairs):
        peer = (own_pair + step) % pairs
        c = pltpu.make_async_remote_copy(
            src_ref=own,
            dst_ref=blocks.at[step],
            send_sem=psend_sem.at[step],
            recv_sem=precv_sem.at[step],
            device_id=(peer, me),
            device_id_type=MESH,
        )
        c.start()
        others.append(c)
    mine = pltpu.make_async_copy(own, all_ref.at[pl.ds(me * tiles, tiles)], local_sem.at[0])
    mine.start()

    def add_block(step):
        source = (own_pair + pairs - step) % pairs
        left = w_ref[:, pl.ds(pl.multiple_of(source * rows, 128), rows)]
        for t in range(tiles):
            right = own[t] if step == 0 else blocks[step, t]
            part = jnp.dot(left, right, preferred_element_type=F32)
            if step == 0:
                cycle_ref[t] = part
            else:
                cycle_ref[t] += part

    w_load.wait()
    add_block(0)
    for step in range(1, n - 1):
        for t in order:
            flying[t, step - 1].wait_recv()
            flying[t, step] = copy_of(step, t)
            flying[t, step].start()
        if step == n - 2:
            for k in range(1, pairs):
                others[k - 1].wait_recv()
                add_block(k)
            cycle_out = pltpu.make_async_copy(cycle_ref, cycle_hbm, local_sem.at[1])
            cycle_out.start()
    for t in order:
        flying[t, n - 2].wait_recv()
    for c in flying.values():
        c.wait_send()
    for c in others:
        c.wait_send()
    mine.wait()
    cycle_out.wait()


def ladder_kernel(table_ref, target_ref, ends_ref, amps_hbm, ints_hbm, out_hbm, amps, held, acc,
                  sem, out_sem):
    count = ints_hbm.shape[0]
    tiles_all = acc.shape[0]
    loads = (
        pltpu.make_async_copy(amps_hbm, amps, sem.at[0]),
        pltpu.make_async_copy(ints_hbm, held.at[pl.ds(0, count)], sem.at[1]),
    )
    for c in loads:
        c.start()
    held[count] = jnp.zeros(held.shape[1:], held.dtype)

    def clear(t, carry):
        acc[t] = jnp.zeros(acc.shape[1:], acc.dtype)
        return carry

    lax.fori_loop(0, tiles_all, clear, 0)
    for c in loads:
        c.wait()

    def step(i, carry):
        for k in range(UNROLL):
            s = i * UNROLL + k
            left = jnp.concatenate(
                [amps[table_ref[1, s * GROUP + g]] for g in range(GROUP)], axis=1
            )
            right = jnp.concatenate(
                [held[table_ref[0, s * GROUP + g]] for g in range(GROUP)], axis=0
            )
            acc[target_ref[s]] += jnp.dot(left, right, preferred_element_type=F32)
        return carry

    def store_of(phase):
        at = pl.ds(pl.multiple_of(phase * PHASE, PHASE), PHASE)
        return pltpu.make_async_copy(acc.at[at], out_hbm.at[at], out_sem.at[phase])

    def run_phase(phase, low):
        high = (ends_ref[(phase + 1) * PHASE - 1] + UNROLL - 1) // UNROLL
        lax.fori_loop(low, high, step, 0)
        store_of(phase).start()
        return high

    def finish(phase, carry):
        store_of(phase).wait()
        return carry

    phases = tiles_all // PHASE
    lax.fori_loop(0, phases, run_phase, jnp.int32(0))
    lax.fori_loop(0, phases, finish, 0)


def reduce_kernel(n, pairs, tiles, keep_ref, cycle_hbm, part_ref, out_ref, cycle_ref, held, sent, sent_scale,
                  got, got_scale, cycle_sem, load_sem, send_sem, recv_sem, ssend_sem, srecv_sem):
    rows = cycle_ref.shape[1]
    width = cycle_ref.shape[2]
    chunks = rows // QROWS
    half = tiles // 2
    order = [t for c in range(half) for t in (c, half + c)]
    own_pair = lax.axis_index("pair")
    place = ring_place(lax.axis_index("ints"), n)

    def slot_of(step, t):
        sign = 1 - 2 * (t * 2 // tiles)
        return ring_index(place + 2 * n - sign * (step + 1), n) * tiles + t

    loads = {}
    for step in range(n):
        for t in order:
            loads[t, step] = pltpu.make_async_copy(
                part_ref.at[slot_of(step, t)], held.at[t, step], load_sem.at[t, step]
            )
            loads[t, step].start()
    cycle_load = pltpu.make_async_copy(cycle_hbm, cycle_ref, cycle_sem)
    cycle_load.start()
    me, own_pair, place, nexts = enter(n, 1)

    def total(step, t, k):
        at = pl.ds(pl.multiple_of(k * QROWS, QROWS), QROWS)
        value = held[t, step, at, :]
        if step > 0:
            scale = got_scale[t, step - 1, pl.ds(k, 1), :]
            value = value + got[t, step - 1, at, :].astype(jnp.int32).astype(F32) * scale
        return at, value

    def pack(step, t):
        def body(k, carry):
            at, value = total(step, t, k)
            top = jnp.maximum(jnp.max(jnp.abs(value), axis=0, keepdims=True), 1e-30)
            sent_scale[t, step, pl.ds(k, 1), :] = top * (1.0 / QMAX)
            scaled = jnp.round(value * (QMAX / top))
            sent[t, step, at, :] = scaled.astype(jnp.int32).astype(jnp.int16)
            return carry

        lax.fori_loop(0, chunks, body, 0)

    def copies(step, t):
        way = t * 2 // tiles
        where = (own_pair, nexts[way])
        return [
            pltpu.make_async_remote_copy(
                src_ref=a.at[t, step], dst_ref=b.at[t, step], send_sem=c.at[t, step],
                recv_sem=d.at[t, step], device_id=where, device_id_type=MESH,
            )
            for a, b, c, d in (
                (sent, got, send_sem, recv_sem),
                (sent_scale, got_scale, ssend_sem, srecv_sem),
            )
        ]

    flying = {}
    for step in range(n - 1):
        for t in order:
            loads[t, step].wait()
            if step > 0:
                for c in flying[t, step - 1]:
                    c.wait_recv()
            pack(step, t)
            flying[t, step] = copies(step, t)
            for c in flying[t, step]:
                c.start()
    cycle_load.wait()
    for t in order:
        loads[t, n - 1].wait()
        for c in flying[t, n - 2]:
            c.wait_recv()
        keep = keep_ref[0, t].astype(F32)

        def body(k, carry):
            at, value = total(n - 1, t, k)
            out_ref[at, t * width:(t + 1) * width] = (value + cycle_ref[t, at, :]) * keep
            return carry

        lax.fori_loop(0, chunks, body, 0)
    for pair_of in flying.values():
        for c in pair_of:
            c.wait_send()


def tables(int_tiles, tiles_all):
    count = int_tiles.shape[0]
    slots = (count + (GROUP - 1) * tiles_all) // GROUP
    slots = (slots + UNROLL - 1) // UNROLL * UNROLL
    u, v = int_tiles[:, 0], int_tiles[:, 1]
    ids = jnp.arange(count, dtype=jnp.int32)
    tile_ids = jnp.arange(tiles_all, dtype=jnp.int32)
    rank = jnp.sum((v[:, None] == v[None, :]) & (ids[None, :] < ids[:, None]), axis=1, dtype=jnp.int32)
    counts = jnp.sum(v[:, None] == tile_ids[None, :], axis=0, dtype=jnp.int32)
    groups = (counts + GROUP - 1) // GROUP
    ends = jnp.sum(jnp.where(tile_ids[:, None] >= tile_ids[None, :], groups[None, :], 0), axis=1)
    base = jnp.sum(jnp.where(tile_ids[None, :] < v[:, None], groups[None, :], 0), axis=1)
    spot = base * GROUP + rank
    hit = spot[None, :] == jnp.arange(slots * GROUP, dtype=jnp.int32)[:, None]
    picks = count + jnp.sum(jnp.where(hit, ids[None, :] - count, 0), axis=1)
    sources = jnp.sum(jnp.where(hit, u[None, :], 0), axis=1)
    target = jnp.sum(ends[None, :] <= jnp.arange(slots, dtype=jnp.int32)[:, None], axis=1, dtype=jnp.int32)
    return jnp.stack([picks, sources]), jnp.minimum(target, tiles_all - 1), ends


def vmem():
    return pl.BlockSpec(memory_space=pltpu.VMEM)


def smem():
    return pl.BlockSpec(memory_space=pltpu.SMEM)


def anywhere():
    return pl.BlockSpec(memory_space=pl.ANY)


def local(n, pairs, t2, t2_live, int_tiles, integrals, cycle_w, res_live):
    rows = t2.shape[0]
    width = integrals.shape[1]
    tiles = t2.shape[1] // width
    tiles_all = tiles * n
    count = integrals.shape[0]
    dma = pltpu.SemaphoreType.DMA
    amps, cycle = pl.pallas_call(
        functools.partial(gather_kernel, n, pairs, tiles),
        out_shape=(
            jax.ShapeDtypeStruct((tiles_all, rows, width), t2.dtype),
            jax.ShapeDtypeStruct((tiles, rows, width), F32),
        ),
        in_specs=[smem(), anywhere(), anywhere()],
        out_specs=(anywhere(), anywhere()),
        scratch_shapes=[
            pltpu.VMEM((tiles, rows, width), t2.dtype),
            pltpu.VMEM((pairs, tiles, rows, width), t2.dtype),
            pltpu.VMEM(t2.shape, t2.dtype),
            pltpu.VMEM(cycle_w.shape, cycle_w.dtype),
            pltpu.VMEM((tiles, rows, width), F32),
            dma((tiles, n)), dma((tiles, n)), dma((pairs,)), dma((pairs,)), dma((3,)),
        ],
        compiler_params=pltpu.CompilerParams(
            collective_id=0, has_side_effects=True, vmem_limit_bytes=48 << 20
        ),
        name="gather_amps",
    )(t2_live, t2, cycle_w)

    table, target, steps = tables(int_tiles, tiles_all)
    partial = pl.pallas_call(
        ladder_kernel,
        out_shape=jax.ShapeDtypeStruct((tiles_all, rows, width), F32),
        in_specs=[smem(), smem(), smem(), anywhere(), anywhere()],
        out_specs=anywhere(),
        scratch_shapes=[
            pltpu.VMEM((tiles_all, rows, width), t2.dtype),
            pltpu.VMEM((count + 1, width, width), integrals.dtype),
            pltpu.VMEM((tiles_all, rows, width), F32),
            dma((2,)), dma((tiles_all // PHASE,)),
        ],
        compiler_params=pltpu.CompilerParams(vmem_limit_bytes=56 << 20),
        name="ladder_partial",
    )(table, target, steps, amps, integrals)

    chunks = rows // QROWS
    return pl.pallas_call(
        functools.partial(reduce_kernel, n, pairs, tiles),
        out_shape=jax.ShapeDtypeStruct((rows, tiles * width), F32),
        in_specs=[smem(), anywhere(), anywhere()],
        out_specs=vmem(),
        scratch_shapes=[
            pltpu.VMEM((tiles, rows, width), F32),
            pltpu.VMEM((tiles, n, rows, width), F32),
            pltpu.VMEM((tiles, n - 1, rows, width), jnp.int16),
            pltpu.VMEM((tiles, n - 1, chunks, width), F32),
            pltpu.VMEM((tiles, n - 1, rows, width), jnp.int16),
            pltpu.VMEM((tiles, n - 1, chunks, width), F32),
            dma, dma((tiles, n)), dma((tiles, n)), dma((tiles, n)), dma((tiles, n)), dma((tiles, n)),
        ],
        compiler_params=pltpu.CompilerParams(
            collective_id=1, has_side_effects=True, vmem_limit_bytes=56 << 20
        ),
        name="reduce_partial",
    )(res_live, cycle, partial)


def solution(mesh):
    n = mesh.shape["ints"]
    pairs = mesh.shape["pair"]
    placed = (
        P("pair", "ints"),
        P("pair", "ints"),
        P("ints", None),
        P("ints", None, None),
        P("pair", None),
        P("pair", "ints"),
    )
    return jax.shard_map(
        functools.partial(local, n, pairs), mesh=mesh, in_specs=placed,
        out_specs=P("pair", "ints"), check_vma=False
    )
```

```python
import functools

import jax
import jax.numpy as jnp
from jax import lax
from jax.experimental import pallas as pl
from jax.experimental.pallas import tpu as pltpu
from jax.sharding import PartitionSpec as P

MESH = pl.DeviceIdType.MESH
QROWS = 64
QMAX = 32766.0
GROUP = 4
UNROLL = 4
PHASE = 4
F32 = jnp.float32


def ring_place(index, n):
    inner = index % 2
    outer = index // 2
    return (1 - inner) * outer + inner * (n - 1 - outer)


def ring_index(place, n):
    place = (place + 2 * n) % n
    half = place // (n // 2)
    return (1 - half) * (2 * place) + half * (2 * (n - 1 - place) + 1)


def enter(n, pairs):
    me = lax.axis_index("ints")
    own_pair = lax.axis_index("pair")
    place = ring_place(me, n)
    nexts = (ring_index(place + 1, n), ring_index(place + n - 1, n))
    barrier = pltpu.get_barrier_semaphore()
    for other in nexts:
        pl.semaphore_signal(barrier, inc=1, device_id=(own_pair, other), device_id_type=MESH)
    for step in range(1, pairs):
        peer = (own_pair + step) % pairs
        pl.semaphore_signal(barrier, inc=1, device_id=(peer, me), device_id_type=MESH)
    pl.semaphore_wait(barrier, 2 + max(pairs - 1, 0))
    return me, own_pair, place, nexts


def gather_kernel(n, pairs, tiles, live_ref, t2_hbm, w_hbm, all_ref, cycle_hbm, own, blocks, t2_ref,
                  w_ref, cycle_ref, send_sem, recv_sem, psend_sem, precv_sem, local_sem):
    rows = t2_ref.shape[0]
    width = t2_ref.shape[1] // tiles
    t2_load = pltpu.make_async_copy(t2_hbm, t2_ref, local_sem.at[1])
    t2_load.start()
    w_load = pltpu.make_async_copy(w_hbm, w_ref, local_sem.at[2])
    w_load.start()
    t2_load.wait()
    for t in range(tiles):
        keep = live_ref[0, t].astype(F32)
        own[t] = (t2_ref[:, t * width:(t + 1) * width].astype(F32) * keep).astype(own.dtype)
    me, own_pair, place, nexts = enter(n, pairs)

    def copy_of(step, t):
        way = t * 2 // tiles
        sign = 1 - 2 * way
        slot = ring_index(place + n - sign * step, n) * tiles + t
        return pltpu.make_async_remote_copy(
            src_ref=own.at[t] if step == 0 else all_ref.at[slot],
            dst_ref=all_ref.at[slot],
            send_sem=send_sem.at[t, step],
            recv_sem=recv_sem.at[t, step],
            device_id=(own_pair, nexts[way]),
            device_id_type=MESH,
        )

    half = tiles // 2
    order = [t for c in range(half) for t in (c, half + c)]
    flying = {}
    for t in order:
        flying[t, 0] = copy_of(0, t)
        flying[t, 0].start()
    others = []
    for step in range(1, pairs):
        peer = (own_pair + step) % pairs
        c = pltpu.make_async_remote_copy(
            src_ref=own,
            dst_ref=blocks.at[step],
            send_sem=psend_sem.at[step],
            recv_sem=precv_sem.at[step],
            device_id=(peer, me),
            device_id_type=MESH,
        )
        c.start()
        others.append(c)
    mine = pltpu.make_async_copy(own, all_ref.at[pl.ds(me * tiles, tiles)], local_sem.at[0])
    mine.start()

    def add_block(step):
        source = (own_pair + pairs - step) % pairs
        left = w_ref[:, pl.ds(pl.multiple_of(source * rows, 128), rows)]
        for t in range(tiles):
            right = own[t] if step == 0 else blocks[step, t]
            part = jnp.dot(left, right, preferred_element_type=F32)
            if step == 0:
                cycle_ref[t] = part
            else:
                cycle_ref[t] += part

    w_load.wait()
    add_block(0)
    for step in range(1, n - 1):
        for t in order:
            flying[t, step - 1].wait_recv()
            flying[t, step] = copy_of(step, t)
            flying[t, step].start()
        if step == n - 2:
            for k in range(1, pairs):
                others[k - 1].wait_recv()
                add_block(k)
            cycle_out = pltpu.make_async_copy(cycle_ref, cycle_hbm, local_sem.at[1])
            cycle_out.start()
    for t in order:
        flying[t, n - 2].wait_recv()
    for c in flying.values():
        c.wait_send()
    for c in others:
        c.wait_send()
    mine.wait()
    cycle_out.wait()


def ladder_kernel(table_hbm, target_hbm, ends_hbm, amps_hbm, ints_hbm, out_hbm, table_ref,
                  target_ref, ends_ref, amps, held, acc, sem, out_sem):
    count = ints_hbm.shape[0]
    tiles_all = acc.shape[0]
    loads = (
        pltpu.make_async_copy(table_hbm, table_ref, sem.at[2]),
        pltpu.make_async_copy(target_hbm, target_ref, sem.at[3]),
        pltpu.make_async_copy(ends_hbm, ends_ref, sem.at[4]),
        pltpu.make_async_copy(amps_hbm, amps, sem.at[0]),
        pltpu.make_async_copy(ints_hbm, held.at[pl.ds(0, count)], sem.at[1]),
    )
    for c in loads:
        c.start()
    held[count] = jnp.zeros(held.shape[1:], held.dtype)

    def clear(t, carry):
        acc[t] = jnp.zeros(acc.shape[1:], acc.dtype)
        return carry

    lax.fori_loop(0, tiles_all, clear, 0)
    for c in loads:
        c.wait()

    def step(i, carry):
        for k in range(UNROLL):
            s = i * UNROLL + k
            left = jnp.concatenate(
                [amps[table_ref[1, s * GROUP + g]] for g in range(GROUP)], axis=1
            )
            right = jnp.concatenate(
                [held[table_ref[0, s * GROUP + g]] for g in range(GROUP)], axis=0
            )
            acc[target_ref[s]] += jnp.dot(left, right, preferred_element_type=F32)
        return carry

    def store_of(phase):
        at = pl.ds(pl.multiple_of(phase * PHASE, PHASE), PHASE)
        return pltpu.make_async_copy(acc.at[at], out_hbm.at[at], out_sem.at[phase])

    def run_phase(phase, low):
        high = (ends_ref[(phase + 1) * PHASE - 1] + UNROLL - 1) // UNROLL
        lax.fori_loop(low, high, step, 0)
        store_of(phase).start()
        return high

    def finish(phase, carry):
        store_of(phase).wait()
        return carry

    phases = tiles_all // PHASE
    lax.fori_loop(0, phases, run_phase, jnp.int32(0))
    lax.fori_loop(0, phases, finish, 0)


def reduce_kernel(n, pairs, tiles, keep_ref, cycle_hbm, part_ref, out_ref, cycle_ref, held, sent, sent_scale,
                  got, got_scale, cycle_sem, load_sem, send_sem, recv_sem, ssend_sem, srecv_sem):
    rows = cycle_ref.shape[1]
    width = cycle_ref.shape[2]
    chunks = rows // QROWS
    half = tiles // 2
    order = [t for c in range(half) for t in (c, half + c)]
    own_pair = lax.axis_index("pair")
    place = ring_place(lax.axis_index("ints"), n)

    def slot_of(step, t):
        sign = 1 - 2 * (t * 2 // tiles)
        return ring_index(place + 2 * n - sign * (step + 1), n) * tiles + t

    loads = {}
    for step in range(n):
        for t in order:
            loads[t, step] = pltpu.make_async_copy(
                part_ref.at[slot_of(step, t)], held.at[t, step], load_sem.at[t, step]
            )
            loads[t, step].start()
    cycle_load = pltpu.make_async_copy(cycle_hbm, cycle_ref, cycle_sem)
    cycle_load.start()

    def total(step, t, k):
        at = pl.ds(pl.multiple_of(k * QROWS, QROWS), QROWS)
        value = held[t, step, at, :]
        if step > 0:
            scale = got_scale[t, step - 1, pl.ds(k, 1), :]
            value = value + got[t, step - 1, at, :].astype(jnp.int32).astype(F32) * scale
        return at, value

    def pack(step, t):
        def body(k, carry):
            at, value = total(step, t, k)
            top = jnp.maximum(jnp.max(jnp.abs(value), axis=0, keepdims=True), 1e-30)
            sent_scale[t, step, pl.ds(k, 1), :] = top * (1.0 / QMAX)
            scaled = jnp.round(value * (QMAX / top))
            sent[t, step, at, :] = scaled.astype(jnp.int32).astype(jnp.int16)
            return carry

        lax.fori_loop(0, chunks, body, 0)

    for t in order:
        loads[t, 0].wait()
        pack(0, t)
    me, own_pair, place, nexts = enter(n, 1)

    def copies(step, t):
        way = t * 2 // tiles
        where = (own_pair, nexts[way])
        return [
            pltpu.make_async_remote_copy(
                src_ref=a.at[t, step], dst_ref=b.at[t, step], send_sem=c.at[t, step],
                recv_sem=d.at[t, step], device_id=where, device_id_type=MESH,
            )
            for a, b, c, d in (
                (sent, got, send_sem, recv_sem),
                (sent_scale, got_scale, ssend_sem, srecv_sem),
            )
        ]

    flying = {}
    for step in range(n - 1):
        for t in order:
            if step > 0:
                loads[t, step].wait()
                for c in flying[t, step - 1]:
                    c.wait_recv()
                pack(step, t)
            flying[t, step] = copies(step, t)
            for c in flying[t, step]:
                c.start()
    cycle_load.wait()
    for t in order:
        loads[t, n - 1].wait()
        for c in flying[t, n - 2]:
            c.wait_recv()
        keep = keep_ref[0, t].astype(F32)

        def body(k, carry):
            at, value = total(n - 1, t, k)
            out_ref[at, t * width:(t + 1) * width] = (value + cycle_ref[t, at, :]) * keep
            return carry

        lax.fori_loop(0, chunks, body, 0)
    for pair_of in flying.values():
        for c in pair_of:
            c.wait_send()


def tables(int_tiles, tiles_all):
    count = int_tiles.shape[0]
    slots = (count + (GROUP - 1) * tiles_all) // GROUP
    slots = (slots + UNROLL - 1) // UNROLL * UNROLL
    u, v = int_tiles[:, 0], int_tiles[:, 1]
    ids = jnp.arange(count, dtype=jnp.int32)
    tile_ids = jnp.arange(tiles_all, dtype=jnp.int32)
    rank = jnp.sum((v[:, None] == v[None, :]) & (ids[None, :] < ids[:, None]), axis=1, dtype=jnp.int32)
    counts = jnp.sum(v[:, None] == tile_ids[None, :], axis=0, dtype=jnp.int32)
    groups = (counts + GROUP - 1) // GROUP
    ends = jnp.sum(jnp.where(tile_ids[:, None] >= tile_ids[None, :], groups[None, :], 0), axis=1)
    base = jnp.sum(jnp.where(tile_ids[None, :] < v[:, None], groups[None, :], 0), axis=1)
    spot = base * GROUP + rank
    hit = spot[None, :] == jnp.arange(slots * GROUP, dtype=jnp.int32)[:, None]
    picks = count + jnp.sum(jnp.where(hit, ids[None, :] - count, 0), axis=1)
    sources = jnp.sum(jnp.where(hit, u[None, :], 0), axis=1)
    target = jnp.sum(ends[None, :] <= jnp.arange(slots, dtype=jnp.int32)[:, None], axis=1, dtype=jnp.int32)
    return jnp.stack([picks, sources]), jnp.minimum(target, tiles_all - 1), ends


def vmem():
    return pl.BlockSpec(memory_space=pltpu.VMEM)


def smem():
    return pl.BlockSpec(memory_space=pltpu.SMEM)


def anywhere():
    return pl.BlockSpec(memory_space=pl.ANY)


def local(n, pairs, t2, t2_live, int_tiles, integrals, cycle_w, res_live):
    rows = t2.shape[0]
    width = integrals.shape[1]
    tiles = t2.shape[1] // width
    tiles_all = tiles * n
    count = integrals.shape[0]
    dma = pltpu.SemaphoreType.DMA
    amps, cycle = pl.pallas_call(
        functools.partial(gather_kernel, n, pairs, tiles),
        out_shape=(
            jax.ShapeDtypeStruct((tiles_all, rows, width), t2.dtype),
            jax.ShapeDtypeStruct((tiles, rows, width), F32),
        ),
        in_specs=[smem(), anywhere(), anywhere()],
        out_specs=(anywhere(), anywhere()),
        scratch_shapes=[
            pltpu.VMEM((tiles, rows, width), t2.dtype),
            pltpu.VMEM((pairs, tiles, rows, width), t2.dtype),
            pltpu.VMEM(t2.shape, t2.dtype),
            pltpu.VMEM(cycle_w.shape, cycle_w.dtype),
            pltpu.VMEM((tiles, rows, width), F32),
            dma((tiles, n)), dma((tiles, n)), dma((pairs,)), dma((pairs,)), dma((3,)),
        ],
        compiler_params=pltpu.CompilerParams(
            collective_id=0, has_side_effects=True, vmem_limit_bytes=48 << 20
        ),
        name="gather_amps",
    )(t2_live, t2, cycle_w)

    table, target, steps = tables(int_tiles, tiles_all)
    partial = pl.pallas_call(
        ladder_kernel,
        out_shape=jax.ShapeDtypeStruct((tiles_all, rows, width), F32),
        in_specs=[anywhere()] * 5,
        out_specs=anywhere(),
        scratch_shapes=[
            pltpu.SMEM(table.shape, table.dtype),
            pltpu.SMEM(target.shape, target.dtype),
            pltpu.SMEM(steps.shape, steps.dtype),
            pltpu.VMEM((tiles_all, rows, width), t2.dtype),
            pltpu.VMEM((count + 1, width, width), integrals.dtype),
            pltpu.VMEM((tiles_all, rows, width), F32),
            dma((5,)), dma((tiles_all // PHASE,)),
        ],
        compiler_params=pltpu.CompilerParams(vmem_limit_bytes=56 << 20),
        name="ladder_partial",
    )(table, target, steps, amps, integrals)

    chunks = rows // QROWS
    return pl.pallas_call(
        functools.partial(reduce_kernel, n, pairs, tiles),
        out_shape=jax.ShapeDtypeStruct((rows, tiles * width), F32),
        in_specs=[smem(), anywhere(), anywhere()],
        out_specs=vmem(),
        scratch_shapes=[
            pltpu.VMEM((tiles, rows, width), F32),
            pltpu.VMEM((tiles, n, rows, width), F32),
            pltpu.VMEM((tiles, n - 1, rows, width), jnp.int16),
            pltpu.VMEM((tiles, n - 1, chunks, width), F32),
            pltpu.VMEM((tiles, n - 1, rows, width), jnp.int16),
            pltpu.VMEM((tiles, n - 1, chunks, width), F32),
            dma, dma((tiles, n)), dma((tiles, n)), dma((tiles, n)), dma((tiles, n)), dma((tiles, n)),
        ],
        compiler_params=pltpu.CompilerParams(
            collective_id=1, has_side_effects=True, vmem_limit_bytes=56 << 20
        ),
        name="reduce_partial",
    )(res_live, cycle, partial)


def solution(mesh):
    n = mesh.shape["ints"]
    pairs = mesh.shape["pair"]
    placed = (
        P("pair", "ints"),
        P("pair", "ints"),
        P("ints", None),
        P("ints", None, None),
        P("pair", None),
        P("pair", "ints"),
    )
    return jax.shard_map(
        functools.partial(local, n, pairs), mesh=mesh, in_specs=placed,
        out_specs=P("pair", "ints"), check_vma=False
    )
```

```python
import functools

import jax
import jax.numpy as jnp
from jax import lax
from jax.experimental import pallas as pl
from jax.experimental.pallas import tpu as pltpu
from jax.sharding import PartitionSpec as P

MESH = pl.DeviceIdType.MESH
QROWS = 64
QMAX = 32766.0
GROUP = 2
UNROLL = 8
PHASE = 4
F32 = jnp.float32


def ring_place(index, n):
    inner = index % 2
    outer = index // 2
    return (1 - inner) * outer + inner * (n - 1 - outer)


def ring_index(place, n):
    place = (place + 2 * n) % n
    half = place // (n // 2)
    return (1 - half) * (2 * place) + half * (2 * (n - 1 - place) + 1)


def enter(n, pairs):
    me = lax.axis_index("ints")
    own_pair = lax.axis_index("pair")
    place = ring_place(me, n)
    nexts = (ring_index(place + 1, n), ring_index(place + n - 1, n))
    barrier = pltpu.get_barrier_semaphore()
    for other in nexts:
        pl.semaphore_signal(barrier, inc=1, device_id=(own_pair, other), device_id_type=MESH)
    for step in range(1, pairs):
        peer = (own_pair + step) % pairs
        pl.semaphore_signal(barrier, inc=1, device_id=(peer, me), device_id_type=MESH)
    pl.semaphore_wait(barrier, 2 + max(pairs - 1, 0))
    return me, own_pair, place, nexts


def gather_kernel(n, pairs, tiles, live_ref, t2_hbm, w_hbm, all_ref, cycle_hbm, own, blocks, t2_ref,
                  w_ref, cycle_ref, send_sem, recv_sem, psend_sem, precv_sem, local_sem):
    rows = t2_ref.shape[0]
    width = t2_ref.shape[1] // tiles
    t2_load = pltpu.make_async_copy(t2_hbm, t2_ref, local_sem.at[1])
    t2_load.start()
    w_load = pltpu.make_async_copy(w_hbm, w_ref, local_sem.at[2])
    w_load.start()
    me, own_pair, place, nexts = enter(n, pairs)
    t2_load.wait()
    for t in range(tiles):
        keep = live_ref[0, t].astype(F32)
        own[t] = (t2_ref[:, t * width:(t + 1) * width].astype(F32) * keep).astype(own.dtype)

    def copy_of(step, t):
        way = t * 2 // tiles
        sign = 1 - 2 * way
        slot = ring_index(place + n - sign * step, n) * tiles + t
        return pltpu.make_async_remote_copy(
            src_ref=own.at[t] if step == 0 else all_ref.at[slot],
            dst_ref=all_ref.at[slot],
            send_sem=send_sem.at[t, step],
            recv_sem=recv_sem.at[t, step],
            device_id=(own_pair, nexts[way]),
            device_id_type=MESH,
        )

    half = tiles // 2
    order = [t for c in range(half) for t in (c, half + c)]
    flying = {}
    for t in order:
        flying[t, 0] = copy_of(0, t)
        flying[t, 0].start()
    others = []
    for step in range(1, pairs):
        peer = (own_pair + step) % pairs
        c = pltpu.make_async_remote_copy(
            src_ref=own,
            dst_ref=blocks.at[step],
            send_sem=psend_sem.at[step],
            recv_sem=precv_sem.at[step],
            device_id=(peer, me),
            device_id_type=MESH,
        )
        c.start()
        others.append(c)
    mine = pltpu.make_async_copy(own, all_ref.at[pl.ds(me * tiles, tiles)], local_sem.at[0])
    mine.start()

    def add_block(step):
        source = (own_pair + pairs - step) % pairs
        left = w_ref[:, pl.ds(pl.multiple_of(source * rows, 128), rows)]
        for t in range(tiles):
            right = own[t] if step == 0 else blocks[step, t]
            part = jnp.dot(left, right, preferred_element_type=F32)
            if step == 0:
                cycle_ref[t] = part
            else:
                cycle_ref[t] += part

    w_load.wait()
    add_block(0)
    for step in range(1, n - 1):
        for t in order:
            flying[t, step - 1].wait_recv()
            flying[t, step] = copy_of(step, t)
            flying[t, step].start()
        if step == n - 2:
            for k in range(1, pairs):
                others[k - 1].wait_recv()
                add_block(k)
            cycle_out = pltpu.make_async_copy(cycle_ref, cycle_hbm, local_sem.at[1])
            cycle_out.start()
    for t in order:
        flying[t, n - 2].wait_recv()
    for c in flying.values():
        c.wait_send()
    for c in others:
        c.wait_send()
    mine.wait()
    cycle_out.wait()


def ladder_kernel(table_ref, target_ref, ends_ref, amps_hbm, ints_hbm, out_hbm, amps, held, acc,
                  sem, out_sem):
    count = ints_hbm.shape[0]
    tiles_all = acc.shape[0]
    loads = (
        pltpu.make_async_copy(amps_hbm, amps, sem.at[0]),
        pltpu.make_async_copy(ints_hbm, held.at[pl.ds(0, count)], sem.at[1]),
    )
    for c in loads:
        c.start()
    held[count] = jnp.zeros(held.shape[1:], held.dtype)

    def clear(t, carry):
        acc[t] = jnp.zeros(acc.shape[1:], acc.dtype)
        return carry

    lax.fori_loop(0, tiles_all, clear, 0)
    for c in loads:
        c.wait()

    def step(i, carry):
        for k in range(UNROLL):
            s = i * UNROLL + k
            left = jnp.concatenate(
                [amps[table_ref[1, s * GROUP + g]] for g in range(GROUP)], axis=1
            )
            right = jnp.concatenate(
                [held[table_ref[0, s * GROUP + g]] for g in range(GROUP)], axis=0
            )
            acc[target_ref[s]] += jnp.dot(left, right, preferred_element_type=F32)
        return carry

    def store_of(phase):
        at = pl.ds(pl.multiple_of(phase * PHASE, PHASE), PHASE)
        return pltpu.make_async_copy(acc.at[at], out_hbm.at[at], out_sem.at[phase])

    def run_phase(phase, low):
        high = (ends_ref[(phase + 1) * PHASE - 1] + UNROLL - 1) // UNROLL
        lax.fori_loop(low, high, step, 0)
        store_of(phase).start()
        return high

    def finish(phase, carry):
        store_of(phase).wait()
        return carry

    phases = tiles_all // PHASE
    lax.fori_loop(0, phases, run_phase, jnp.int32(0))
    lax.fori_loop(0, phases, finish, 0)


def reduce_kernel(n, pairs, tiles, keep_ref, cycle_hbm, part_ref, out_ref, cycle_ref, held, sent, sent_scale,
                  got, got_scale, cycle_sem, load_sem, send_sem, recv_sem, ssend_sem, srecv_sem):
    rows = cycle_ref.shape[1]
    width = cycle_ref.shape[2]
    chunks = rows // QROWS
    half = tiles // 2
    order = [t for c in range(half) for t in (c, half + c)]
    own_pair = lax.axis_index("pair")
    place = ring_place(lax.axis_index("ints"), n)

    def slot_of(step, t):
        sign = 1 - 2 * (t * 2 // tiles)
        return ring_index(place + 2 * n - sign * (step + 1), n) * tiles + t

    loads = {}
    for step in range(n):
        for t in order:
            loads[t, step] = pltpu.make_async_copy(
                part_ref.at[slot_of(step, t)], held.at[t, step], load_sem.at[t, step]
            )
            loads[t, step].start()
    cycle_load = pltpu.make_async_copy(cycle_hbm, cycle_ref, cycle_sem)
    cycle_load.start()
    me, own_pair, place, nexts = enter(n, 1)

    def total(step, t, k):
        at = pl.ds(pl.multiple_of(k * QROWS, QROWS), QROWS)
        value = held[t, step, at, :]
        if step > 0:
            scale = got_scale[t, step - 1, pl.ds(k, 1), :]
            value = value + got[t, step - 1, at, :].astype(jnp.int32).astype(F32) * scale
        return at, value

    def pack(step, t):
        def body(k, carry):
            at, value = total(step, t, k)
            top = jnp.maximum(jnp.max(jnp.abs(value), axis=0, keepdims=True), 1e-30)
            sent_scale[t, step, pl.ds(k, 1), :] = top * (1.0 / QMAX)
            scaled = jnp.round(value * (QMAX / top))
            sent[t, step, at, :] = scaled.astype(jnp.int32).astype(jnp.int16)
            return carry

        lax.fori_loop(0, chunks, body, 0)

    def copies(step, t):
        way = t * 2 // tiles
        where = (own_pair, nexts[way])
        return [
            pltpu.make_async_remote_copy(
                src_ref=a.at[t, step], dst_ref=b.at[t, step], send_sem=c.at[t, step],
                recv_sem=d.at[t, step], device_id=where, device_id_type=MESH,
            )
            for a, b, c, d in (
                (sent, got, send_sem, recv_sem),
                (sent_scale, got_scale, ssend_sem, srecv_sem),
            )
        ]

    flying = {}
    for step in range(n - 1):
        for t in order:
            loads[t, step].wait()
            if step > 0:
                for c in flying[t, step - 1]:
                    c.wait_recv()
            pack(step, t)
            flying[t, step] = copies(step, t)
            for c in flying[t, step]:
                c.start()
    cycle_load.wait()
    for t in order:
        loads[t, n - 1].wait()
        for c in flying[t, n - 2]:
            c.wait_recv()
        keep = keep_ref[0, t].astype(F32)

        def body(k, carry):
            at, value = total(n - 1, t, k)
            out_ref[at, t * width:(t + 1) * width] = (value + cycle_ref[t, at, :]) * keep
            return carry

        lax.fori_loop(0, chunks, body, 0)
    for pair_of in flying.values():
        for c in pair_of:
            c.wait_send()


def tables(int_tiles, tiles_all):
    count = int_tiles.shape[0]
    slots = (count + (GROUP - 1) * tiles_all) // GROUP
    slots = (slots + UNROLL - 1) // UNROLL * UNROLL
    u, v = int_tiles[:, 0], int_tiles[:, 1]
    ids = jnp.arange(count, dtype=jnp.int32)
    tile_ids = jnp.arange(tiles_all, dtype=jnp.int32)
    rank = jnp.sum((v[:, None] == v[None, :]) & (ids[None, :] < ids[:, None]), axis=1, dtype=jnp.int32)
    counts = jnp.sum(v[:, None] == tile_ids[None, :], axis=0, dtype=jnp.int32)
    groups = (counts + GROUP - 1) // GROUP
    ends = jnp.sum(jnp.where(tile_ids[:, None] >= tile_ids[None, :], groups[None, :], 0), axis=1)
    base = jnp.sum(jnp.where(tile_ids[None, :] < v[:, None], groups[None, :], 0), axis=1)
    spot = base * GROUP + rank
    hit = spot[None, :] == jnp.arange(slots * GROUP, dtype=jnp.int32)[:, None]
    picks = count + jnp.sum(jnp.where(hit, ids[None, :] - count, 0), axis=1)
    sources = jnp.sum(jnp.where(hit, u[None, :], 0), axis=1)
    target = jnp.sum(ends[None, :] <= jnp.arange(slots, dtype=jnp.int32)[:, None], axis=1, dtype=jnp.int32)
    return jnp.stack([picks, sources]), jnp.minimum(target, tiles_all - 1), ends


def vmem():
    return pl.BlockSpec(memory_space=pltpu.VMEM)


def smem():
    return pl.BlockSpec(memory_space=pltpu.SMEM)


def anywhere():
    return pl.BlockSpec(memory_space=pl.ANY)


def local(n, pairs, t2, t2_live, int_tiles, integrals, cycle_w, res_live):
    rows = t2.shape[0]
    width = integrals.shape[1]
    tiles = t2.shape[1] // width
    tiles_all = tiles * n
    count = integrals.shape[0]
    dma = pltpu.SemaphoreType.DMA
    amps, cycle = pl.pallas_call(
        functools.partial(gather_kernel, n, pairs, tiles),
        out_shape=(
            jax.ShapeDtypeStruct((tiles_all, rows, width), t2.dtype),
            jax.ShapeDtypeStruct((tiles, rows, width), F32),
        ),
        in_specs=[smem(), anywhere(), anywhere()],
        out_specs=(anywhere(), anywhere()),
        scratch_shapes=[
            pltpu.VMEM((tiles, rows, width), t2.dtype),
            pltpu.VMEM((pairs, tiles, rows, width), t2.dtype),
            pltpu.VMEM(t2.shape, t2.dtype),
            pltpu.VMEM(cycle_w.shape, cycle_w.dtype),
            pltpu.VMEM((tiles, rows, width), F32),
            dma((tiles, n)), dma((tiles, n)), dma((pairs,)), dma((pairs,)), dma((3,)),
        ],
        compiler_params=pltpu.CompilerParams(
            collective_id=0, has_side_effects=True, vmem_limit_bytes=48 << 20
        ),
        name="gather_amps",
    )(t2_live, t2, cycle_w)

    table, target, steps = tables(int_tiles, tiles_all)
    partial = pl.pallas_call(
        ladder_kernel,
        out_shape=jax.ShapeDtypeStruct((tiles_all, rows, width), F32),
        in_specs=[smem(), smem(), smem(), anywhere(), anywhere()],
        out_specs=anywhere(),
        scratch_shapes=[
            pltpu.VMEM((tiles_all, rows, width), t2.dtype),
            pltpu.VMEM((count + 1, width, width), integrals.dtype),
            pltpu.VMEM((tiles_all, rows, width), F32),
            dma((2,)), dma((tiles_all // PHASE,)),
        ],
        compiler_params=pltpu.CompilerParams(vmem_limit_bytes=56 << 20),
        name="ladder_partial",
    )(table, target, steps, amps, integrals)

    chunks = rows // QROWS
    return pl.pallas_call(
        functools.partial(reduce_kernel, n, pairs, tiles),
        out_shape=jax.ShapeDtypeStruct((rows, tiles * width), F32),
        in_specs=[smem(), anywhere(), anywhere()],
        out_specs=vmem(),
        scratch_shapes=[
            pltpu.VMEM((tiles, rows, width), F32),
            pltpu.VMEM((tiles, n, rows, width), F32),
            pltpu.VMEM((tiles, n - 1, rows, width), jnp.int16),
            pltpu.VMEM((tiles, n - 1, chunks, width), F32),
            pltpu.VMEM((tiles, n - 1, rows, width), jnp.int16),
            pltpu.VMEM((tiles, n - 1, chunks, width), F32),
            dma, dma((tiles, n)), dma((tiles, n)), dma((tiles, n)), dma((tiles, n)), dma((tiles, n)),
        ],
        compiler_params=pltpu.CompilerParams(
            collective_id=1, has_side_effects=True, vmem_limit_bytes=56 << 20
        ),
        name="reduce_partial",
    )(res_live, cycle, partial)


def solution(mesh):
    n = mesh.shape["ints"]
    pairs = mesh.shape["pair"]
    placed = (
        P("pair", "ints"),
        P("pair", "ints"),
        P("ints", None),
        P("ints", None, None),
        P("pair", None),
        P("pair", "ints"),
    )
    return jax.shard_map(
        functools.partial(local, n, pairs), mesh=mesh, in_specs=placed,
        out_specs=P("pair", "ints"), check_vma=False
    )
```
